512 devices in a mesh: dp: 16 (over y, x_hi, core), blk: 32 (over x_lo, z).
Axes of the slice: x: 4 (x_hi: 2, x_lo: 2; x = x_hi * 2 + x_lo), y: 4, z: 16, core: 2. Of those that a mesh axis runs over, the one named last changes fastest.
Arguments:
- pre_gelu: bfloat16 [98304, 4096], P(('dp', 'blk')), may hold values from -8 to 8
- out_grad: bfloat16 [98304, 1024], P(('dp', 'blk')), may hold values from -6 to 6
- down_weight: bfloat16 [4096, 1024], P('blk'), may hold values from -0.09375 to 0.09375
Outputs:
- block_out: bfloat16 [98304, 1024], P(('dp', 'blk'))
- pre_grad: bfloat16 [98304, 4096], P(('dp', 'blk'))
- weight_grad: float32 [4096, 1024], P('blk')
The draws below stay inside these ranges and needn't reach their ends.
All inputs are finite; a program needn't handle non-finite values.
Results may differ from the reference program's by a relative error of at most 0.017.
Values may be sent and summed in bfloat16 or wider, within the bound.
A program may use at most 64 MiB of HBM per device.

```python
import math
import jax
import jax.numpy as jnp
from jax import lax

D = 1024
FF = 4096
ROWS_DEV = 192
TOKENS = 98304
N_DP = 16
N_BLK = 32


def steps_of(own_key, dims, shards, least, largest):
    def one(position, shards_of):
        draws = jax.random.uniform(jax.random.fold_in(jax.random.fold_in(own_key, 6), position), (shards_of,), jnp.float32, least / len(shards), largest / len(shards))
        return jnp.repeat(jnp.exp(draws), dims[position] // shards_of).reshape((-1,) + (1,) * (len(dims) - position - 1))

    loudness = one(*shards[0])
    for cut in shards[1:]:
        loudness = loudness * one(*cut)
    return loudness


def bell_draw(stream_key, extent, scale, limit, cuts=(), kind=jnp.bfloat16):
    values = scale * jax.random.normal(stream_key, extent, jnp.float32)
    if cuts:
        values = values * steps_of(stream_key, extent, cuts, -0.22, 0.18)
    return jnp.clip(values, -limit, limit).astype(kind)


def setup_inputs(seed: int = 0) -> dict:
    streams_of = jax.random.split(jax.random.key(seed), 4)
    return {
        "pre_gelu": bell_draw(streams_of[0], (TOKENS, FF), 1.5, 8.0, ((0, 512),)),
        "out_grad": bell_draw(streams_of[1], (TOKENS, D), 1.0, 6.0, ((0, 512),)),
        "down_weight": bell_draw(streams_of[2], (FF, D), FF ** -0.5, 0.09375, ((0, 32),)),
    }


SQRT_TWO_PI = 0.7978845608028654
CUBIC = 0.044715

def gelu_parts(inputs):
    argument = SQRT_TWO_PI * (inputs + CUBIC * inputs * inputs * inputs)
    tangent = jnp.tanh(argument)
    activation = 0.5 * inputs * (1.0 + tangent)
    derivative = 0.5 * (1.0 + tangent) + 0.5 * inputs * (1.0 - tangent * tangent) * SQRT_TWO_PI * (1.0 + 3.0 * CUBIC * inputs * inputs)
    return (activation, derivative)

def group_pass(pre_group, grad_group, down_weight):
    activation, derivative = gelu_parts(pre_group.astype(jnp.float32))
    hidden = activation.astype(jnp.bfloat16)
    output = jnp.dot(hidden, down_weight, preferred_element_type=jnp.float32).astype(jnp.bfloat16)
    d_hidden = jnp.dot(grad_group, down_weight.T, preferred_element_type=jnp.float32)
    pre_grad = (d_hidden * derivative).astype(jnp.bfloat16)
    blocks = FF // N_BLK
    stacked = hidden.reshape(N_BLK, ROWS_DEV, N_BLK, blocks)
    targets = grad_group.reshape(N_BLK, ROWS_DEV, D)
    diagonal = jnp.arange(N_BLK)

    def add_stop(accumulated, offset):
        shifted = jnp.roll(stacked, -offset, axis=0)[diagonal, :, diagonal, :]
        paired = jnp.roll(targets, -offset, axis=0)
        contribution = jnp.einsum('brf,brd->bfd', shifted.astype(jnp.float32), paired.astype(jnp.float32))
        return ((accumulated.astype(jnp.float32) + contribution).astype(jnp.bfloat16), offset)
    initial = jnp.zeros((N_BLK, blocks, D), jnp.bfloat16)
    accumulated = lax.scan(add_stop, initial, jnp.arange(1, N_BLK + 1, dtype=jnp.int32))[0]
    return (output, pre_grad, accumulated.reshape(FF, D))

def reference(pre_gelu, out_grad, down_weight):
    groups_pre = pre_gelu.reshape(N_DP, N_BLK * ROWS_DEV, FF)
    groups_grad = out_grad.reshape(N_DP, N_BLK * ROWS_DEV, D)

    def per_group(summed, pieces):
        output, pre_grad, accumulated = group_pass(pieces[0], pieces[1], down_weight)
        return (summed + accumulated.astype(jnp.float32), (output, pre_grad))
    summed, results = lax.scan(per_group, jnp.zeros((FF, D), jnp.float32), (groups_pre, groups_grad))
    weight_grad = summed / math.sqrt(TOKENS)
    return (results[0].reshape(TOKENS, D), results[1].reshape(TOKENS, FF), weight_grad)
```

```python
import math

import jax
import jax.numpy as jnp
from jax import lax
from jax.experimental import pallas as pl
from jax.experimental.pallas import tpu as pltpu
from jax.sharding import PartitionSpec as P

MESH = pl.DeviceIdType.MESH
SQRT_TWO_PI = 0.7978845608028654
CUBIC = 0.044715
F32, BF16 = jnp.float32, jnp.bfloat16
R = 192
D = 1024
BLK = 128
HALF = 64
SHARE = 2048


def gelu_parts(inputs):
    squared = inputs * inputs
    argument = inputs * (SQRT_TWO_PI + (SQRT_TWO_PI * CUBIC) * squared)
    tangent = jnp.tanh(argument)
    gate = 0.5 + 0.5 * tangent
    activation = inputs * gate
    bend = inputs * (0.5 * SQRT_TWO_PI + (1.5 * CUBIC * SQRT_TWO_PI) * squared)
    derivative = gate + (1.0 - tangent * tangent) * bend
    return activation, derivative


def kernel(
    pre_ref, og_ref, w_ref, bo_ref, pg_ref, wgrad_ref,
    xs, hs, ss, gs, wg, ts, ry, rx, rz, acc, bor, pgs, fr, fo,
    in_sem, agd_r, agy_r, agz_s, agx_s, agy_s, rsy_s, rsd_s, rsy_r, rsx_r, rsz_r,
    pgl_sem, pgs_sem, pgr_sem, bo_sem, f1_s, f1_r, f2_s, f2_r,
):
    dp = lax.axis_index("dp")
    blk = lax.axis_index("blk")
    y, xh, c = dp // 4, (dp // 2) % 2, dp % 2
    xl, z = blk // 16, blk % 16
    x = xh * 2 + xl
    yp = y % 2
    q = y * 2 + xh
    is_src = c == xl
    is_sink = c != xl

    def dev(x, y, z, c):
        x, y, z = (x + 4) % 4, (y + 4) % 4, (z + 16) % 16
        return (y * 4 + (x // 2) * 2 + c, (x % 2) * 16 + z)

    sibling = dev(x, y, z, 1 - c)

    def remote(src, dst, send, recv, device):
        return pltpu.make_async_remote_copy(
            src_ref=src, dst_ref=dst, send_sem=send, recv_sem=recv, device_id=device, device_id_type=MESH
        )

    z_cols = pl.ds(pl.multiple_of(yp * 256, 128), 768)
    x_cols = pl.ds(pl.multiple_of(yp * 384, 128), 640)
    src_own, src_other = (pl.ds(pl.multiple_of(k * 768, 128), 256) for k in (yp, 1 - yp))
    sink_own, sink_other = (pl.ds(pl.multiple_of(k * 640, 128), 384) for k in (yp, 1 - yp))

    mine = pl.ds(pl.multiple_of(c * SHARE, SHARE), SHARE)
    theirs = pl.ds(pl.multiple_of((1 - c) * SHARE, SHARE), SHARE)
    load_x = pltpu.make_async_copy(pre_ref.at[:, mine], xs.at[pl.ds(0, R)], in_sem.at[0])
    load_g = pltpu.make_async_copy(og_ref, gs.at[pl.ds(0, R)], in_sem.at[1])
    load_w = pltpu.make_async_copy(w_ref.at[:, z_cols], wg.at[0, pl.ds(0, BLK), z_cols], in_sem.at[2])

    @pl.when(is_src)
    def _():
        load_w.start()

    load_x.start()
    load_g.start()

    barrier = pltpu.get_barrier_semaphore()
    peers = [dev(x, y, z + 1, c), dev(x, y, z - 1, c), dev(x + 1, y, z, c), dev(x - 1, y, z, c), sibling]
    for dy in range(4):
        for dx in (0, 2):
            if dy or dx:
                peers += [dev(x + dx, y + dy, z, c), dev(x + dx, y + dy, z, 1 - c)]
    for peer in peers:
        pl.semaphore_signal(barrier, inc=1, device_id=peer, device_id_type=MESH)
    pl.semaphore_wait(barrier, len(peers))

    swap_x = remote(pre_ref.at[:, theirs], xs.at[pl.ds(R, R)], in_sem.at[3], in_sem.at[4], sibling)
    swap_g = remote(og_ref, gs.at[pl.ds(R, R)], in_sem.at[5], in_sem.at[6], sibling)

    def rows(side, half):
        return pl.ds(side * BLK + half * HALF, HALF)

    def unit(p, side, half):
        return 4 * p + 2 * side + half

    def z_to(side):
        return dev(x, y, z + 1 - 2 * side, c)

    def ag_z(p, side, half, to_p, to_side, way):
        u = unit(to_p, to_side, half)
        return remote(
            wg.at[p, rows(side, half), z_cols], wg.at[to_p, rows(to_side, half), z_cols],
            agz_s.at[u], agd_r.at[u], z_to(way),
        )

    def ag_x(p, side, half):
        u, at = unit(p, side, half), wg.at[p, rows(side, half), x_cols]
        return remote(at, at, agx_s.at[u], agd_r.at[u], dev(x + 1 - 2 * half, y, z, c))

    def ag_y(p, side, half, cols):
        u, at = unit(p, side, half), wg.at[p, rows(side, half), cols]
        return remote(at, at, agy_s.at[u], agy_r.at[u], dev(x, y + 1 - 2 * half, z, c))

    def ag_src(d, half):
        for side in (0, 1):
            ag_z(d, side, half, d, side, side).wait_recv()

            @pl.when(d < 7)
            def _():
                ag_z(d, side, half, d + 1, side, side).start()

            @pl.when((d == 7) & (half == side))
            def _():
                ag_z(d, side, half, 0, 1, side).start()

            ag_x(d, side, half).start()
            ag_y(d, side, half, src_own).start()

    def ag_src_last(half):
        ag_z(0, 1, half, 0, 1, half).wait_recv()
        ag_x(0, 1, half).start()
        ag_y(0, 1, half, src_own).start()

    def ag_sink(p, half, sides=(0, 1)):
        for side in sides:
            ag_x(p, side, half).wait_recv()
            ag_y(p, side, half, sink_own).start()

    def ag_step(m):
        d, half = 1 + m // 2, m % 2
        pl.when(is_src)(lambda: ag_src(d, half))
        pl.when(is_sink)(lambda: ag_sink(d, half))

    def rs_y(p, side, half, cols):
        u = unit(p, side, half)
        return remote(
            ts.at[p, rows(side, half), cols], ry.at[p, rows(side, half), cols],
            rsy_s.at[u], rsy_r.at[u], dev(x, y - 1 + 2 * half, z, c),
        )

    def rs_x(p, side, half):
        u = unit(p, side, half)
        return remote(
            ts.at[p, rows(side, half), x_cols], rx.at[p, rows(side, half), x_cols],
            rsd_s.at[u], rsx_r.at[u], dev(x - 1 + 2 * half, y, z, c),
        )

    def rs_z(p, side, half, to_p, to_side, way):
        u = unit(p, side, half)
        return remote(
            ts.at[p, rows(side, half), z_cols], rz.at[to_p, rows(to_side, half), z_cols],
            rsd_s.at[u], rsz_r.at[unit(to_p, to_side, half)], z_to(1 - way),
        )

    def add(p, at, cols, buffer, from_at=None):
        from_at = at if from_at is None else from_at
        ts[p, at, cols] = ts[p, at, cols] + buffer[p, from_at, cols]

    def rs_y_send(p):
        for side in (0, 1):
            for half in (0, 1):
                pl.when(is_src)(lambda: rs_y(p, side, half, src_other).start())
                pl.when(is_sink)(lambda: rs_y(p, side, half, sink_other).start())

    def rs_sink(p, side, half):
        rs_y(p, side, half, sink_own).wait_recv()
        add(p, rows(side, half), sink_own, ry)
        rs_x(p, side, half).start()

    def rs_local(p, side, half):
        rs_y(p, side, half, src_own).wait_recv()
        add(p, rows(side, half), src_own, ry)
        rs_x(p, side, half).wait_recv()
        add(p, rows(side, half), x_cols, rx)

    def rs_src(p, side, half):
        rs_local(p, side, half)

        @pl.when((p < 7) | (half != side))
        def _():
            rs_z(p, side, half, p, side, side).wait_recv()
            add(p, rows(side, half), z_cols, rz)

        rs_z(p, side, half, p - 1, side, side).start()

    def rs_src_first(half):
        rs_local(0, 1, half)
        rs_z(0, 1, half, 7, 1 - half, 1 - half).start()

    def block_columns(p, side):
        far = jnp.where(p == 0, 8, p)
        zb = (z + far) % 16 if side else (z - p + 16) % 16
        return pl.multiple_of(zb * BLK, BLK)

    def hidden_and_term(p):
        for side in (0, 1):
            cols = pl.ds(block_columns(p, side), BLK)

            @pl.loop(0, 2 * R // 64)
            def _(i):
                at = pl.ds(pl.multiple_of(i * 64, 64), 64)
                activation, derivative = gelu_parts(xs[at, cols].astype(F32))
                hs[p, at, pl.ds(side * BLK, BLK)] = activation.astype(BF16)
                ss[p, at, pl.ds(side * BLK, BLK)] = derivative

        turned = hs[p].T
        for n in range(4):
            cols = pl.ds(n * 256, 256)
            ts[p, :, cols] = jnp.dot(turned, gs[:, cols], preferred_element_type=F32).astype(BF16)

    def pg_copy(p, side, own):
        cols = pl.ds(pl.multiple_of(c * SHARE, SHARE) + block_columns(p, side), BLK)
        part = pgs.at[p, pl.ds(0 if own else R, R), pl.ds(side * BLK, BLK)]
        k = 2 * p + side
        if own:
            return pltpu.make_async_copy(part, pg_ref.at[:, cols], pgl_sem.at[k])
        return remote(part, pg_ref.at[:, cols], pgs_sem.at[k], pgr_sem.at[k], sibling)

    def use_weight(p, first):
        for side in (0, 1):
            for half in (0, 1):
                pl.when(is_src)(lambda: ag_y(p, side, half, src_other).wait_recv())
                pl.when(is_sink)(lambda: ag_y(p, side, half, sink_other).wait_recv())
        weight = wg.at[p]
        d_hidden = lax.dot_general(gs[...], weight[...], (((1,), (1,)), ((), ())), preferred_element_type=F32)
        pgs[p] = (d_hidden * ss[p]).astype(BF16)
        for side in (0, 1):
            pg_copy(p, side, False).start()
            pg_copy(p, side, True).start()
        for n in range(4):
            cols = pl.ds(n * 256, 256)
            product = jnp.dot(hs[p], weight[:, cols], preferred_element_type=F32)
            acc[:, cols] = product if first else acc[:, cols] + product

    swap_x.start()
    swap_g.start()

    @pl.when(is_src)
    def _():
        load_w.wait()
        for half in (0, 1):
            ag_z(0, 0, half, 1, 0, 0).start()
            ag_z(0, 0, half, 1, 1, 1).start()
        for half in (0, 1):
            ag_x(0, 0, half).start()
            ag_y(0, 0, half, src_own).start()

    load_x.wait()
    load_g.wait()
    swap_x.wait_recv()
    swap_g.wait_recv()

    @pl.loop(0, 8)
    def _(s):
        p = (8 - s) % 8
        hidden_and_term(p)
        rs_y_send(p)

        @pl.when((s == 1) & is_sink)
        def _():
            for half in (0, 1):
                ag_sink(0, half, (0,))

        @pl.when(s >= 2)
        def _():
            ag_step(s - 2)

        @pl.when((s >= 2) & is_sink)
        def _():
            before = (10 - s) % 8
            for half in (0, 1):
                for side in (0, 1):
                    rs_sink(before, side, half)

    @pl.loop(0, 8)
    def _(k):
        @pl.when((k < 2) & is_sink)
        def _():
            for half in (0, 1):
                for side in (0, 1):
                    rs_sink(2 - k, side, half)

        @pl.when((k == 0) & is_src)
        def _():
            for half in (0, 1):
                rs_src_first(half)

        ag_step(6 + k)

        @pl.when((k > 0) & is_src)
        def _():
            for half in (0, 1):
                for side in (0, 1):
                    rs_src(8 - k, side, half)

        @pl.when(k == 1)
        def _():
            use_weight(1, True)

        @pl.when(k > 1)
        def _():
            use_weight(k, False)

    def chip(k):
        return (k % 2) * 2 + xl, k // 2

    def f1(k, sender):
        far_x, far_y = chip(k)
        cols = z_cols
        return remote(
            ts.at[0, pl.ds(16 * k, 16), cols], fr.at[sender, :, cols], f1_s.at[k], f1_r.at[sender], dev(far_x, far_y, z, c)
        )

    def f2(k, core):
        far_x, far_y = chip(k)
        at = fo.at[pl.ds(pl.multiple_of(16 * q, 16), 16)]
        return remote(at, at, f2_s.at[2 * k + core], f2_r.at[q], dev(far_x, far_y, z, core))

    def f2_arrival(k):
        at = fo.at[pl.ds(16 * k, 16)]
        return remote(at, at, f2_s.at[2 * k], f2_r.at[k], sibling)

    @pl.when(is_src)
    def _():
        for half in (0, 1):
            ag_src_last(half)
        for half in (0, 1):
            rs_local(0, 0, half)
            for side in (0, 1):
                rs_z(1, side, half, 0, side, side).wait_recv()
                add(0, rows(0, half), z_cols, rz, rows(side, half))
        for k in range(8):

            @pl.when(q != k)
            def _():
                f1(k, q).start()

    @pl.when(is_sink)
    def _():
        for half in (0, 1):
            ag_sink(0, half, (1,))

    @pl.when(is_src)
    def _():
        own_rows = pl.ds(pl.multiple_of(16 * q, 16), 16)
        fr[q, :, z_cols] = ts[0, own_rows, z_cols]
        for k in range(8):

            @pl.when(q != k)
            def _():
                even = k // 2 % 2 == 0
                cols = pl.ds(0 if even else 256, 768)
                remote(fr.at[k, :, cols], fr.at[k, :, cols], f1_s.at[k], f1_r.at[k], sibling).wait_recv()

        def total(keys, cols):
            return sum(fr[k, :, cols].astype(F32) for k in keys)

        even, odd = (0, 1, 4, 5), (2, 3, 6, 7)
        fo[own_rows, pl.ds(0, 256)] = total(even, pl.ds(0, 256)).astype(BF16)
        fo[own_rows, pl.ds(256, 512)] = total(even + odd, pl.ds(256, 512)).astype(BF16)
        fo[own_rows, pl.ds(768, 256)] = total(odd, pl.ds(768, 256)).astype(BF16)
        for k in range(8):
            for core in (0, 1):

                @pl.when((q != k) | (c != core))
                def _():
                    f2(k, core).start()

    use_weight(0, False)
    theirs_out = remote(acc.at[pl.ds(R, R)], bor, bo_sem.at[0], bo_sem.at[1], sibling)
    theirs_out.start()
    for k in range(8):

        @pl.when((q != k) | is_sink)
        def _():
            f2_arrival(k).wait_recv()

    wgrad_ref[...] = fo[...].astype(F32) * (1.0 / math.sqrt(98304))
    theirs_out.wait_recv()
    bo_ref[...] = (acc[pl.ds(0, R)] + bor[...]).astype(BF16)

    swap_x.wait_send()
    swap_g.wait_send()
    theirs_out.wait_send()

    @pl.loop(0, 8)
    def _(p):
        for side in (0, 1):
            pg_copy(p, side, True).wait()
            pg_copy(p, side, False).wait()
            for half in (0, 1):

                @pl.when(is_src)
                def _():
                    ag_x(p, side, half).wait_send()
                    ag_y(p, side, half, src_own).wait_send()
                    rs_y(p, side, half, src_other).wait_send()

                    @pl.when((p > 0) | (side == 1))
                    def _():
                        ag_z(p, side, half, p, side, side).wait_send()
                        rs_z(p, side, half, p, side, side).wait_send()

                @pl.when(is_sink)
                def _():
                    ag_y(p, side, half, sink_own).wait_send()
                    rs_y(p, side, half, sink_other).wait_send()
                    rs_x(p, side, half).wait_send()

    @pl.when(is_src)
    def _():
        for k in range(8):

            @pl.when(q != k)
            def _():
                f1(k, q).wait_send()

            for core in (0, 1):

                @pl.when((q != k) | (c != core))
                def _():
                    f2(k, core).wait_send()


def body(pre_gelu, out_grad, down_weight):
    dma = pltpu.SemaphoreType.DMA
    vmem = pltpu.VMEM
    hbm = pl.BlockSpec(memory_space=pl.ANY)
    return pl.pallas_call(
        kernel,
        out_shape=(
            jax.ShapeDtypeStruct((R, D), BF16),
            jax.ShapeDtypeStruct((R, 2 * SHARE), BF16),
            jax.ShapeDtypeStruct((BLK, D), F32),
        ),
        in_specs=[hbm, hbm, hbm],
        out_specs=(
            pl.BlockSpec(memory_space=vmem),
            hbm,
            pl.BlockSpec(memory_space=vmem),
        ),
        scratch_shapes=[
            vmem((2 * R, SHARE), BF16),
            vmem((8, 2 * R, 256), BF16),
            vmem((8, 2 * R, 256), F32),
            vmem((2 * R, D), BF16),
            vmem((8, 256, D), BF16),
            vmem((8, 256, D), BF16),
            vmem((8, 256, D), BF16),
            vmem((8, 256, D), BF16),
            vmem((8, 256, D), BF16),
            vmem((2 * R, D), F32),
            vmem((R, D), F32),
            vmem((8, 2 * R, 256), BF16),
            vmem((8, 16, D), BF16),
            vmem((BLK, D), BF16),
            dma((7,)),
            *[dma((32,)) for _ in range(10)],
            dma((16,)),
            dma((16,)),
            dma((16,)),
            dma((2,)),
            dma((8,)),
            dma((8,)),
            dma((16,)),
            dma((8,)),
        ],
        compiler_params=pltpu.CompilerParams(
            collective_id=0, has_side_effects=True, vmem_limit_bytes=56 * 1024 * 1024
        ),
        cost_estimate=pl.CostEstimate(flops=4831838208, bytes_accessed=4 << 20, transcendentals=786432),
        name="fused",
    )(pre_gelu, out_grad, down_weight)


def solution(mesh):
    in_specs = (P(("dp", "blk"), None), P(("dp", "blk"), None), P("blk", None))
    out_specs = (P(("dp", "blk"), None), P(("dp", "blk"), None), P("blk", None))
    return jax.shard_map(body, mesh=mesh, in_specs=in_specs, out_specs=out_specs, check_vma=False)
```

```python
import math

import jax
import jax.numpy as jnp
from jax import lax
from jax.experimental import pallas as pl
from jax.experimental.pallas import tpu as pltpu
from jax.sharding import PartitionSpec as P

MESH = pl.DeviceIdType.MESH
SQRT_TWO_PI = 0.7978845608028654
CUBIC = 0.044715
F32, BF16 = jnp.float32, jnp.bfloat16
R = 192
D = 1024
BLK = 128
HALF = 64
SHARE = 2048


def gelu_parts(inputs):
    squared = inputs * inputs
    argument = inputs * (SQRT_TWO_PI + (SQRT_TWO_PI * CUBIC) * squared)
    tangent = jnp.tanh(argument)
    gate = 0.5 + 0.5 * tangent
    activation = inputs * gate
    bend = inputs * (0.5 * SQRT_TWO_PI + (1.5 * CUBIC * SQRT_TWO_PI) * squared)
    derivative = gate + (1.0 - tangent * tangent) * bend
    return activation, derivative


def kernel(
    pre_ref, og_ref, w_ref, bo_ref, pg_ref, fo,
    xs, hs, ss, gs, wg, ts, ry, rx, rz, acc, bor, pgs, fr,
    in_sem, sx_s, sx_r, agd_r, agy_r, agz_s, agx_s, agy_s, rsy_s, rsd_s, rsy_r, rsx_r, rsz_r,
    pgs_sem, pgr_sem, bo_sem, f1_s, f1_r, f2_s, f2_r,
):
    dp = lax.axis_index("dp")
    blk = lax.axis_index("blk")
    y, xh, c = dp // 4, (dp // 2) % 2, dp % 2
    xl, z = blk // 16, blk % 16
    x = xh * 2 + xl
    yp = y % 2
    q = y * 2 + xh
    is_src = c == xl
    is_sink = c != xl

    def dev(x, y, z, c):
        x, y, z = (x + 4) % 4, (y + 4) % 4, (z + 16) % 16
        return (y * 4 + (x // 2) * 2 + c, (x % 2) * 16 + z)

    sibling = dev(x, y, z, 1 - c)

    def remote(src, dst, send, recv, device):
        return pltpu.make_async_remote_copy(
            src_ref=src, dst_ref=dst, send_sem=send, recv_sem=recv, device_id=device, device_id_type=MESH
        )

    z_cols = pl.ds(pl.multiple_of(yp * 256, 128), 768)
    x_cols = pl.ds(pl.multiple_of(yp * 384, 128), 640)
    src_own, src_other = (pl.ds(pl.multiple_of(k * 768, 128), 256) for k in (yp, 1 - yp))
    sink_own, sink_other = (pl.ds(pl.multiple_of(k * 640, 128), 384) for k in (yp, 1 - yp))

    mine = pl.ds(pl.multiple_of(c * SHARE, SHARE), SHARE)
    load_x = pltpu.make_async_copy(pre_ref.at[:, mine], xs.at[pl.ds(0, R)], in_sem.at[0])
    load_g = pltpu.make_async_copy(og_ref, gs.at[pl.ds(0, R)], in_sem.at[1])
    load_w = pltpu.make_async_copy(w_ref.at[:, z_cols], wg.at[0, pl.ds(0, BLK), z_cols], in_sem.at[2])

    @pl.when(is_src)
    def _():
        load_w.start()

    load_x.start()
    load_g.start()

    acc[...] = jnp.zeros_like(acc)
    barrier = pltpu.get_barrier_semaphore()
    peers = [dev(x, y, z + 1, c), dev(x, y, z - 1, c), dev(x + 1, y, z, c), dev(x - 1, y, z, c), sibling]
    for dy in range(4):
        for dx in (0, 2):
            if dy or dx:
                peers += [dev(x + dx, y + dy, z, c), dev(x + dx, y + dy, z, 1 - c)]
    for peer in peers:
        pl.semaphore_signal(barrier, inc=1, device_id=peer, device_id_type=MESH)
    pl.semaphore_wait(barrier, len(peers))

    def block_columns(p, side):
        far = jnp.where(p == 0, 8, p)
        zb = (z + far) % 16 if side else (z - p + 16) % 16
        return pl.multiple_of(zb * BLK, BLK)

    swap_g = remote(og_ref, gs.at[pl.ds(R, R)], in_sem.at[3], in_sem.at[4], sibling)

    def swap_x(p, side):
        at, k = block_columns(p, side), 2 * p + side
        theirs = pl.ds(pl.multiple_of((1 - c) * SHARE, SHARE) + at, BLK)
        return remote(pre_ref.at[:, theirs], xs.at[pl.ds(R, R), pl.ds(at, BLK)], sx_s.at[k], sx_r.at[k], sibling)

    def rows(side, half):
        return pl.ds(side * BLK + half * HALF, HALF)

    def unit(p, side, half):
        return 4 * p + 2 * side + half

    def z_to(side):
        return dev(x, y, z + 1 - 2 * side, c)

    def ag_z(p, side, half, to_p, to_side, way):
        u = unit(to_p, to_side, half)
        return remote(
            wg.at[p, rows(side, half), z_cols], wg.at[to_p, rows(to_side, half), z_cols],
            agz_s.at[u], agd_r.at[u], z_to(way),
        )

    def ag_x(p, side, half):
        u, at = unit(p, side, half), wg.at[p, rows(side, half), x_cols]
        return remote(at, at, agx_s.at[u], agd_r.at[u], dev(x + 1 - 2 * half, y, z, c))

    def ag_y(p, side, half, cols):
        u, at = unit(p, side, half), wg.at[p, rows(side, half), cols]
        return remote(at, at, agy_s.at[u], agy_r.at[u], dev(x, y + 1 - 2 * half, z, c))

    def ag_src(d, half):
        for side in (0, 1):
            ag_z(d, side, half, d, side, side).wait_recv()

            @pl.when(d < 7)
            def _():
                ag_z(d, side, half, d + 1, side, side).start()

            @pl.when((d == 7) & (half == side))
            def _():
                ag_z(d, side, half, 0, 1, side).start()

            ag_x(d, side, half).start()
            ag_y(d, side, half, src_own).start()

    def ag_src_last(half):
        ag_z(0, 1, half, 0, 1, half).wait_recv()
        ag_x(0, 1, half).start()
        ag_y(0, 1, half, src_own).start()

    def ag_sink(p, half, sides=(0, 1)):
        for side in sides:
            ag_x(p, side, half).wait_recv()
            ag_y(p, side, half, sink_own).start()

    def ag_step(m):
        d, half = 1 + m // 2, m % 2
        pl.when(is_src)(lambda: ag_src(d, half))
        pl.when(is_sink)(lambda: ag_sink(d, half))

    def rs_y(p, side, half, cols):
        u = unit(p, side, half)
        return remote(
            ts.at[p, rows(side, half), cols], ry.at[p, rows(side, half), cols],
            rsy_s.at[u], rsy_r.at[u], dev(x, y - 1 + 2 * half, z, c),
        )

    def rs_x(p, side, half):
        u = unit(p, side, half)
        return remote(
            ts.at[p, rows(side, half), x_cols], rx.at[p, rows(side, half), x_cols],
            rsd_s.at[u], rsx_r.at[u], dev(x - 1 + 2 * half, y, z, c),
        )

    def rs_z(p, side, half, to_p, to_side, way):
        u = unit(p, side, half)
        return remote(
            ts.at[p, rows(side, half), z_cols], rz.at[to_p, rows(to_side, half), z_cols],
            rsd_s.at[u], rsz_r.at[unit(to_p, to_side, half)], z_to(1 - way),
        )

    def add(p, at, cols, buffer, from_at=None):
        from_at = at if from_at is None else from_at
        ts[p, at, cols] = ts[p, at, cols] + buffer[p, from_at, cols]

    def rs_y_send(p):
        for side in (0, 1):
            for half in (0, 1):
                pl.when(is_src)(lambda: rs_y(p, side, half, src_other).start())
                pl.when(is_sink)(lambda: rs_y(p, side, half, sink_other).start())

    def rs_sink(p, side, half):
        rs_y(p, side, half, sink_own).wait_recv()
        add(p, rows(side, half), sink_own, ry)
        rs_x(p, side, half).start()

    def rs_local(p, side, half):
        rs_y(p, side, half, src_own).wait_recv()
        add(p, rows(side, half), src_own, ry)
        rs_x(p, side, half).wait_recv()
        add(p, rows(side, half), x_cols, rx)

    def rs_src(p, side, half):
        @pl.when((p < 7) | (half != side))
        def _():
            rs_z(p, side, half, p, side, side).wait_recv()
            add(p, rows(side, half), z_cols, rz)

        rs_z(p, side, half, p - 1, side, side).start()

    def rs_src_first(half):
        rs_local(0, 1, half)
        rs_z(0, 1, half, 7, 1 - half, 1 - half).start()

    def hidden(p):
        for side in (0, 1):
            cols = pl.ds(block_columns(p, side), BLK)

            @pl.loop(0, 2 * R // 64)
            def _(i):
                at = pl.ds(pl.multiple_of(i * 64, 64), 64)
                activation, derivative = gelu_parts(xs[at, cols].astype(F32))
                hs[p, at, pl.ds(side * BLK, BLK)] = activation.astype(BF16)
                ss[p, at, pl.ds(side * BLK, BLK)] = derivative

    def term(p):
        turned = hs[p].T
        for n in range(4):
            cols = pl.ds(n * 256, 256)
            ts[p, :, cols] = jnp.dot(turned, gs[:, cols], preferred_element_type=F32).astype(BF16)

    def pg_columns(p, side):
        return pl.ds(pl.multiple_of(c * SHARE, SHARE) + block_columns(p, side), BLK)

    def pg_copy(p, side):
        k = 2 * p + side
        part = pgs.at[p, :, pl.ds(side * BLK, BLK)]
        return remote(part, pg_ref.at[:, pg_columns(p, side)], pgs_sem.at[k], pgr_sem.at[k], sibling)

    theirs_out = remote(acc.at[pl.ds(R, R)], bor, bo_sem.at[0], bo_sem.at[1], sibling)

    def use_weight(p, last=False):
        for side in (0, 1):
            for half in (0, 1):
                pl.when(is_src)(lambda: ag_y(p, side, half, src_other).wait_recv())
                pl.when(is_sink)(lambda: ag_y(p, side, half, sink_other).wait_recv())
        weight = wg.at[p]

        def add_out(at):
            for n in range(4):
                cols = pl.ds(n * 256, 256)
                acc[at, cols] += jnp.dot(hs[p, at, :], weight[:, cols], preferred_element_type=F32)

        if last:
            add_out(pl.ds(R, R))
            theirs_out.start()
        d_hidden = lax.dot_general(gs[...], weight[...], (((1,), (1,)), ((), ())), preferred_element_type=F32)
        grads = (d_hidden * ss[p]).astype(BF16)
        pgs[p] = grads[R:]
        for side in (0, 1):
            pg_copy(p, side).start()
        for side in (0, 1):
            pg_ref[:, pg_columns(p, side)] = grads[:R, side * BLK : (side + 1) * BLK]
        add_out(pl.ds(0, R) if last else pl.ds(0, 2 * R))

    @pl.when(is_src)
    def _():
        load_w.wait()
        for half in (0, 1):
            ag_z(0, 0, half, 1, 0, 0).start()
            ag_z(0, 0, half, 1, 1, 1).start()

    swap_x(0, 0).start()
    swap_x(0, 1).start()
    swap_g.start()

    @pl.loop(1, 8)
    def _(s):
        swap_x(8 - s, 0).start()
        swap_x(8 - s, 1).start()

    @pl.when(is_src)
    def _():
        for half in (0, 1):
            ag_x(0, 0, half).start()
            ag_y(0, 0, half, src_own).start()

    load_x.wait()
    load_g.wait()

    @pl.loop(0, 8)
    def _(s):
        p = (8 - s) % 8
        swap_x(p, 0).wait_recv()
        swap_x(p, 1).wait_recv()
        hidden(p)

        @pl.when(s == 0)
        def _():
            swap_g.wait_recv()

        term(p)
        rs_y_send(p)

        @pl.when((s == 1) & is_sink)
        def _():
            for half in (0, 1):
                ag_sink(0, half, (0,))

        @pl.when((s >= 2) & is_sink)
        def _():
            before = (10 - s) % 8
            for half in (0, 1):
                for side in (0, 1):
                    rs_sink(before, side, half)

        @pl.when(s >= 2)
        def _():
            ag_step(s - 2)

        @pl.when((s == 6) & is_src)
        def _():
            for half in (0, 1):
                rs_src_first(half)

    @pl.when(is_src)
    def _():
        for side in (0, 1):
            rs_local(7, side, 0)

    @pl.loop(2, 16)
    def _(n):
        @pl.when(is_src)
        def _():
            for side in (0, 1):
                rs_src(8 - n // 2, side, n % 2)
            later = 7 - (n - 1) // 2
            rs_local(later, 0, (n + 1) % 2)

            @pl.when(later > 0)
            def _():
                rs_local(later, 1, (n + 1) % 2)

        @pl.when((n < 4) & is_sink)
        def _():
            for half in (0, 1):
                for side in (0, 1):
                    rs_sink(4 - n, side, half)

        @pl.when((n < 13) & ((n - 2) % 3 < 2))
        def _():
            ag_step(n + 4 - (n - 2) // 3)

        @pl.when((n == 14) & is_src)
        def _():
            for half in (0, 1):
                ag_src_last(half)

        @pl.when((n % 2 == 1) & (n < 14))
        def _():
            use_weight(n // 2)

    def chip(k):
        return (k % 2) * 2 + xl, k // 2

    def f1(k, sender):
        far_x, far_y = chip(k)
        return remote(
            ts.at[0, pl.ds(16 * k, 16), z_cols], fr.at[sender, :, z_cols],
            f1_s.at[k], f1_r.at[sender], dev(far_x, far_y, z, c),
        )

    def f1_arrival(k):
        at = fr.at[k, :, pl.ds(0 if k // 2 % 2 == 0 else 256, 768)]
        return remote(at, at, f1_s.at[k], f1_r.at[k], sibling)

    def f2(k, core):
        far_x, far_y = chip(k)
        at = fo.at[pl.ds(pl.multiple_of(16 * q, 16), 16)]
        return remote(at, at, f2_s.at[2 * k + core], f2_r.at[q], dev(far_x, far_y, z, core))

    def f2_arrival(k):
        at = fo.at[pl.ds(16 * k, 16)]
        return remote(at, at, f2_s.at[2 * k], f2_r.at[k], sibling)

    @pl.when(is_src)
    def _():
        for half in (0, 1):
            if half:
                rs_local(0, 0, half)
            for side in (0, 1):
                rs_z(1, side, half, 0, side, side).wait_recv()
                add(0, rows(0, half), z_cols, rz, rows(side, half))
            for k in range(4 * half, 4 * half + 4):

                @pl.when(q != k)
                def _():
                    f1(k, q).start()

    @pl.when(is_sink)
    def _():
        for half in (0, 1):
            ag_sink(0, half, (1,))

    use_weight(7)

    @pl.when(is_src)
    def _():
        own_rows = pl.ds(pl.multiple_of(16 * q, 16), 16)
        fr[q, :, z_cols] = ts[0, own_rows, z_cols]
        for k in range(8):
            pl.when(q != k)(lambda: f1_arrival(k).wait_recv())

        def total(keys, cols):
            return sum(fr[k, :, cols].astype(F32) for k in keys)

        even, odd = (0, 1, 4, 5), (2, 3, 6, 7)
        fo[own_rows, pl.ds(0, 256)] = total(even, pl.ds(0, 256)).astype(BF16)
        fo[own_rows, pl.ds(256, 512)] = total(even + odd, pl.ds(256, 512)).astype(BF16)
        fo[own_rows, pl.ds(768, 256)] = total(odd, pl.ds(768, 256)).astype(BF16)
        for k in range(8):
            for core in (0, 1):

                @pl.when((q != k) | (c != core))
                def _():
                    f2(k, core).start()

    use_weight(0, True)

    swap_g.wait_send()

    @pl.loop(0, 8)
    def _(p):
        for side in (0, 1):
            swap_x(p, side).wait_send()
            pg_copy(p, side).wait()
            for half in (0, 1):

                @pl.when(is_src)
                def _():
                    ag_x(p, side, half).wait_send()
                    ag_y(p, side, half, src_own).wait_send()
                    rs_y(p, side, half, src_other).wait_send()

                    @pl.when((p > 0) | (side == 1))
                    def _():
                        ag_z(p, side, half, p, side, side).wait_send()
                        rs_z(p, side, half, p, side, side).wait_send()

                @pl.when(is_sink)
                def _():
                    ag_y(p, side, half, sink_own).wait_send()
                    rs_y(p, side, half, sink_other).wait_send()
                    rs_x(p, side, half).wait_send()

    theirs_out.wait()
    bo_ref[...] = (acc[pl.ds(0, R)] + bor[...]).astype(BF16)

    @pl.when(is_src)
    def _():
        for k in range(8):
            pl.when(q != k)(lambda: f1(k, q).wait_send())
            for core in (0, 1):

                @pl.when((q != k) | (c != core))
                def _():
                    f2(k, core).wait_send()

    for k in range(8):

        @pl.when((q != k) | is_sink)
        def _():
            f2_arrival(k).wait_recv()


def finish(bo_ref, pg_ref, fo_ref, bo_out, pg_out, wgrad_out, scaled, sem):
    copies = [
        pltpu.make_async_copy(pg_ref, pg_out, sem.at[0]),
        pltpu.make_async_copy(bo_ref, bo_out, sem.at[1]),
        pltpu.make_async_copy(scaled, wgrad_out, sem.at[2]),
    ]
    copies[0].start()
    copies[1].start()
    scaled[...] = fo_ref[...].astype(F32) * (1.0 / math.sqrt(98304))
    copies[2].start()
    for copy in copies:
        copy.wait()


def body(pre_gelu, out_grad, down_weight):
    dma = pltpu.SemaphoreType.DMA
    vmem = pltpu.VMEM
    hbm = pl.BlockSpec(memory_space=pl.ANY)
    whole = pl.BlockSpec(memory_space=vmem)
    results = pl.pallas_call(
        kernel,
        out_shape=(
            jax.ShapeDtypeStruct((R, D), BF16),
            jax.ShapeDtypeStruct((R, 2 * SHARE), BF16),
            jax.ShapeDtypeStruct((BLK, D), BF16),
        ),
        in_specs=[pl.BlockSpec(memory_space=pltpu.HBM)] * 3,
        out_specs=(whole, whole, whole),
        scratch_shapes=[
            vmem((2 * R, SHARE), BF16),
            vmem((8, 2 * R, 256), BF16),
            vmem((8, 2 * R, 256), F32),
            vmem((2 * R, D), BF16),
            vmem((8, 256, D), BF16),
            vmem((8, 256, D), BF16),
            vmem((8, 256, D), BF16),
            vmem((8, 256, D), BF16),
            vmem((8, 256, D), BF16),
            vmem((2 * R, D), F32),
            vmem((R, D), F32),
            vmem((8, R, 256), BF16),
            vmem((8, 16, D), BF16),
            dma((5,)),
            dma((16,)),
            dma((16,)),
            *[dma((32,)) for _ in range(10)],
            dma((16,)),
            dma((16,)),
            dma((2,)),
            dma((8,)),
            dma((8,)),
            dma((16,)),
            dma((8,)),
        ],
        compiler_params=pltpu.CompilerParams(
            collective_id=0, has_side_effects=True, vmem_limit_bytes=50 * 1024 * 1024
        ),
        cost_estimate=pl.CostEstimate(flops=4831838208, bytes_accessed=4 << 20, transcendentals=786432),
        name="fused",
    )(pre_gelu, out_grad, down_weight)
    return pl.pallas_call(
        finish,
        out_shape=(
            jax.ShapeDtypeStruct((R, D), BF16),
            jax.ShapeDtypeStruct((R, 2 * SHARE), BF16),
            jax.ShapeDtypeStruct((BLK, D), F32),
        ),
        in_specs=[whole, whole, whole],
        out_specs=(hbm, hbm, hbm),
        scratch_shapes=[vmem((BLK, D), F32), dma((3,))],
        compiler_params=pltpu.CompilerParams(vmem_limit_bytes=4 * 1024 * 1024),
        cost_estimate=pl.CostEstimate(flops=131072, bytes_accessed=3 << 20, transcendentals=0),
        name="finish",
    )(*results)


def solution(mesh):
    in_specs = (P(("dp", "blk"), None), P(("dp", "blk"), None), P("blk", None))
    out_specs = (P(("dp", "blk"), None), P(("dp", "blk"), None), P("blk", None))
    return jax.shard_map(body, mesh=mesh, in_specs=in_specs, out_specs=out_specs, check_vma=False)
```

```python
import math

import jax
import jax.numpy as jnp
from jax import lax
from jax.experimental import pallas as pl
from jax.experimental.pallas import tpu as pltpu
from jax.sharding import PartitionSpec as P

MESH = pl.DeviceIdType.MESH
SQRT_TWO_PI = 0.7978845608028654
CUBIC = 0.044715
F32, BF16 = jnp.float32, jnp.bfloat16
R = 192
D = 1024
BLK = 128
HALF = 64
AG_PARTS = 1
RS_PARTS = 2
SHARE = 2048


def gelu_parts(inputs):
    squared = inputs * inputs
    argument = inputs * (SQRT_TWO_PI + (SQRT_TWO_PI * CUBIC) * squared)
    tangent = jnp.tanh(argument)
    gate = 0.5 + 0.5 * tangent
    activation = inputs * gate
    bend = inputs * (0.5 * SQRT_TWO_PI + (1.5 * CUBIC * SQRT_TWO_PI) * squared)
    derivative = gate + (1.0 - tangent * tangent) * bend
    return activation, derivative


def kernel(
    pre_ref, og_ref, w_ref, bo_ref, pg_ref, fo,
    xs, hs, ss, gs, wg, ts, ry, rx, rz, acc, bor, pgs, fr,
    in_sem, sx_s, sx_r, agx_r, agy_r, agx_s, agy_s, rsy_s, rsx_s, rsy_r, rsx_r, agz_s, agz_r, rsz_s, rsz_r,
    pgs_sem, pgr_sem, bo_sem, f1_s, f1_r, f2_s, f2_r,
):
    dp = lax.axis_index("dp")
    blk = lax.axis_index("blk")
    y, xh, c = dp // 4, (dp // 2) % 2, dp % 2
    xl, z = blk // 16, blk % 16
    yp = y % 2
    q = y * 2 + xh
    is_src = c == xl
    is_sink = c != xl

    z_next = [(dp, xl * 16 + (z + 1) % 16), (dp, xl * 16 + (z + 15) % 16)]
    x_same, x_flip = xh * 2, (1 - xh) * 2
    x_blk = (1 - xl) * 16 + z
    x_next = [
        (y * 4 + jnp.where(xl == 0, x_same, x_flip) + c, x_blk),
        (y * 4 + jnp.where(xl == 0, x_flip, x_same) + c, x_blk),
    ]
    y_next = [((y + 1) % 4 * 4 + dp % 4, blk), ((y + 3) % 4 * 4 + dp % 4, blk)]
    sibling = (dp + 1 - 2 * c, blk)

    def pick(pair, down):
        if isinstance(down, int):
            return pair[down]
        return tuple(jnp.where(down == 0, a, b) for a, b in zip(*pair))

    def remote(src, dst, send, recv, device):
        return pltpu.make_async_remote_copy(
            src_ref=src, dst_ref=dst, send_sem=send, recv_sem=recv, device_id=device, device_id_type=MESH
        )

    z_cols = pl.ds(pl.multiple_of(yp * 384, 128), 640)
    x_cols = pl.ds(pl.multiple_of(yp * 384, 128), 640)
    src_own, src_other = (pl.ds(pl.multiple_of(k * 640, 128), 384) for k in (yp, 1 - yp))
    sink_own, sink_other = (pl.ds(pl.multiple_of(k * 640, 128), 384) for k in (yp, 1 - yp))

    mine = pl.ds(pl.multiple_of(c * SHARE, SHARE), SHARE)
    load_x = pltpu.make_async_copy(pre_ref.at[:, mine], xs.at[pl.ds(0, R)], in_sem.at[0])
    load_g = pltpu.make_async_copy(og_ref, gs.at[pl.ds(0, R)], in_sem.at[1])
    load_w = pltpu.make_async_copy(w_ref.at[:, z_cols], wg.at[0, pl.ds(0, BLK), z_cols], in_sem.at[2])

    @pl.when(is_src)
    def _():
        load_w.start()

    load_x.start()
    load_g.start()

    acc[...] = jnp.zeros_like(acc)
    barrier = pltpu.get_barrier_semaphore()
    for peer in z_next + x_next:
        pl.semaphore_signal(barrier, inc=1, device_id=peer, device_id_type=MESH)
    for k in range(16):

        @pl.when(dp != k)
        def _():
            pl.semaphore_signal(barrier, inc=1, device_id=(k, blk), device_id_type=MESH)

    pl.semaphore_wait(barrier, 19)

    def block_columns(p, side):
        far = jnp.where(p == 0, 8, p)
        zb = (z + far) % 16 if side else (z - p + 16) % 16
        return pl.multiple_of(zb * BLK, BLK)

    swap_g = remote(og_ref, gs.at[pl.ds(R, R)], in_sem.at[3], in_sem.at[4], sibling)

    def swap_x(p, side):
        at, k = block_columns(p, side), 2 * p + side
        theirs = pl.ds(pl.multiple_of((1 - c) * SHARE, SHARE) + at, BLK)
        return remote(pre_ref.at[:, theirs], xs.at[pl.ds(R, R), pl.ds(at, BLK)], sx_s.at[k], sx_r.at[k], sibling)

    def rows(side, half):
        return pl.ds(side * BLK + half * HALF, HALF)

    def part_rows(side, half, part, parts):
        return pl.ds(side * BLK + half * HALF + part * (HALF // parts), HALF // parts)

    def unit(p, side, half):
        return 4 * p + 2 * side + half

    def z_to(side):
        return z_next[side]

    def ag_z(p, side, half, to_p, to_side, way, part):
        u = AG_PARTS * unit(to_p, to_side, half) + part
        return remote(
            wg.at[p, part_rows(side, half, part, AG_PARTS), z_cols],
            wg.at[to_p, part_rows(to_side, half, part, AG_PARTS), z_cols],
            agz_s.at[u], agz_r.at[u], z_to(way),
        )

    def ag_x(p, side, half):
        u, at = unit(p, side, half), wg.at[p, rows(side, half), x_cols]
        return remote(at, at, agx_s.at[u], agx_r.at[u], pick(x_next, half))

    def ag_y(p, side, half, cols):
        u, at = unit(p, side, half), wg.at[p, rows(side, half), cols]
        return remote(at, at, agy_s.at[u], agy_r.at[u], pick(y_next, half))

    def ag_src(d, half):
        for part in range(AG_PARTS):
            for side in (0, 1):
                ag_z(d, side, half, d, side, side, part).wait_recv()

                @pl.when(d < 7)
                def _():
                    ag_z(d, side, half, d + 1, side, side, part).start()

                @pl.when((d == 7) & (half == side))
                def _():
                    ag_z(d, side, half, 0, 1, side, part).start()

        for side in (0, 1):
            ag_x(d, side, half).start()
            ag_y(d, side, half, src_own).start()

    def ag_src_last(half):
        for part in range(AG_PARTS):
            ag_z(0, 1, half, 0, 1, half, part).wait_recv()
        ag_x(0, 1, half).start()
        ag_y(0, 1, half, src_own).start()

    def ag_sink(p, half, sides=(0, 1)):
        for side in sides:
            ag_x(p, side, half).wait_recv()
            ag_y(p, side, half, sink_own).start()

    def rs_y(p, side, half, cols):
        u = unit(p, side, half)
        return remote(
            ts.at[p, rows(side, half), cols], ry.at[p, rows(side, half), cols],
            rsy_s.at[u], rsy_r.at[u], pick(y_next, 1 - half),
        )

    def rs_x(p, side, half):
        u = unit(p, side, half)
        return remote(
            ts.at[p, rows(side, half), x_cols], rx.at[p, rows(side, half), x_cols],
            rsx_s.at[u], rsx_r.at[u], pick(x_next, 1 - half),
        )

    def rs_z(p, side, half, to_p, to_side, way, part):
        return remote(
            ts.at[p, part_rows(side, half, part, RS_PARTS), z_cols],
            rz.at[to_p, part_rows(to_side, half, part, RS_PARTS), z_cols],
            rsz_s.at[RS_PARTS * unit(p, side, half) + part],
            rsz_r.at[RS_PARTS * unit(to_p, to_side, half) + part], z_to(1 - way),
        )

    def add(p, at, cols, buffer, from_at=None):
        from_at = at if from_at is None else from_at
        ts[p, at, cols] = ts[p, at, cols] + buffer[p, from_at, cols]

    def rs_y_send(p):
        def send(cols):
            for side in (0, 1):
                for half in (0, 1):
                    rs_y(p, side, half, cols).start()

        pl.when(is_src)(lambda: send(src_other))
        pl.when(is_sink)(lambda: send(sink_other))

    def rs_sink(p, side, half):
        rs_y(p, side, half, sink_own).wait_recv()
        add(p, rows(side, half), sink_own, ry)
        rs_x(p, side, half).start()

    def rs_local(p, side, half):
        rs_y(p, side, half, src_own).wait_recv()
        add(p, rows(side, half), src_own, ry)
        rs_x(p, side, half).wait_recv()
        add(p, rows(side, half), x_cols, rx)

    def rs_src(p, half):
        for part in range(RS_PARTS):
            for side in (0, 1):

                @pl.when((p < 7) | (half != side))
                def _():
                    rs_z(p, side, half, p, side, side, part).wait_recv()
                    add(p, part_rows(side, half, part, RS_PARTS), z_cols, rz)

                rs_z(p, side, half, p - 1, side, side, part).start()

    def rs_src_first(half):
        rs_local(0, 1, half)
        for part in range(RS_PARTS):
            rs_z(0, 1, half, 7, 1 - half, 1 - half, part).start()

    def hidden(p):
        for side in (0, 1):
            cols = pl.ds(block_columns(p, side), BLK)

            @pl.loop(0, 2 * R // 64)
            def _(i):
                at = pl.ds(pl.multiple_of(i * 64, 64), 64)
                activation, derivative = gelu_parts(xs[at, cols].astype(F32))
                hs[p, at, pl.ds(side * BLK, BLK)] = activation.astype(BF16)
                ss[p, at, pl.ds(side * BLK, BLK)] = derivative

    def term(p):
        turned = hs[p].T
        for n in range(4):
            cols = pl.ds(n * 256, 256)
            ts[p, :, cols] = jnp.dot(turned, gs[:, cols], preferred_element_type=F32).astype(BF16)

    def pg_columns(p, side):
        return pl.ds(pl.multiple_of(c * SHARE, SHARE) + block_columns(p, side), BLK)

    def pg_copy(p, side):
        k = 2 * p + side
        part = pgs.at[p, :, pl.ds(side * BLK, BLK)]
        return remote(part, pg_ref.at[:, pg_columns(p, side)], pgs_sem.at[k], pgr_sem.at[k], sibling)

    theirs_out = remote(acc.at[pl.ds(R, R)], bor, bo_sem.at[0], bo_sem.at[1], sibling)

    def use_weight(p, last=False):
        def arrive(cols):
            for side in (0, 1):
                for half in (0, 1):
                    ag_y(p, side, half, cols).wait_recv()

        pl.when(is_src)(lambda: arrive(src_other))
        pl.when(is_sink)(lambda: arrive(sink_other))
        weight = wg.at[p]

        def add_out(at):
            for n in range(4):
                cols = pl.ds(n * 256, 256)
                acc[at, cols] += jnp.dot(hs[p, at, :], weight[:, cols], preferred_element_type=F32)

        if last:
            add_out(pl.ds(R, R))
            theirs_out.start()
        d_hidden = lax.dot_general(gs[...], weight[...], (((1,), (1,)), ((), ())), preferred_element_type=F32)
        grads = (d_hidden * ss[p]).astype(BF16)
        pgs[p] = grads[R:]
        for side in (0, 1):
            pg_copy(p, side).start()
        for side in (0, 1):
            pg_ref[:, pg_columns(p, side)] = grads[:R, side * BLK : (side + 1) * BLK]
        add_out(pl.ds(0, R) if last else pl.ds(0, 2 * R))

    @pl.when(is_src)
    def _():
        load_w.wait()
        for half in (0, 1):
            for part in range(AG_PARTS):
                ag_z(0, 0, half, 1, 0, 0, part).start()
                ag_z(0, 0, half, 1, 1, 1, part).start()

    swap_x(0, 0).start()
    swap_x(0, 1).start()
    swap_g.start()

    @pl.loop(1, 8)
    def _(s):
        swap_x(8 - s, 0).start()
        swap_x(8 - s, 1).start()

    @pl.when(is_src)
    def _():
        for half in (0, 1):
            ag_x(0, 0, half).start()
            ag_y(0, 0, half, src_own).start()

    load_x.wait()
    load_g.wait()

    @pl.loop(0, 8)
    def _(s):
        p = (8 - s) % 8
        swap_x(p, 0).wait_recv()
        swap_x(p, 1).wait_recv()
        hidden(p)

        @pl.when(s == 0)
        def _():
            swap_g.wait_recv()

        term(p)
        rs_y_send(p)

        @pl.when((s >= 2) & is_sink)
        def _():
            before = (10 - s) % 8
            for half in (0, 1):
                for side in (0, 1):
                    rs_sink(before, side, half)

        @pl.when((s == 6) & is_src)
        def _():
            for half in (0, 1):
                rs_src_first(half)

        @pl.when((s > 2) & (s % 2 == 1) & is_src)
        def _():
            m = (s - 3) // 2
            ag_src(1 + m // 2, m % 2)

        @pl.when((s == 5) & is_sink)
        def _():
            for half in (0, 1):
                ag_sink(0, half, (0,))

        @pl.when((s == 7) & is_sink)
        def _():
            ag_sink(1, 0)

    @pl.when(is_src)
    def _():
        for side in (0, 1):
            rs_local(7, side, 0)

    @pl.loop(2, 16)
    def _(n):
        @pl.when(is_src)
        def _():
            rs_src(8 - n // 2, n % 2)
            later = 7 - (n - 1) // 2
            rs_local(later, 0, (n + 1) % 2)

            @pl.when(later > 0)
            def _():
                rs_local(later, 1, (n + 1) % 2)

        @pl.when((n < 4) & is_sink)
        def _():
            for half in (0, 1):
                for side in (0, 1):
                    rs_sink(4 - n, side, half)

        @pl.when((n < 13) & is_src)
        def _():
            ag_src((n + 3) // 2, (n + 1) % 2)

        @pl.when((n < 15) & is_sink)
        def _():
            ag_sink((n + 1) // 2, (n + 1) % 2)

        @pl.when((n == 14) & is_src)
        def _():
            for half in (0, 1):
                ag_src_last(half)

        @pl.when((n % 2 == 1) & (n > 4))
        def _():
            use_weight((n - 3) // 2)

    def f1(k, sender):
        return remote(
            ts.at[0, pl.ds(16 * k, 16), z_cols], fr.at[sender, :, z_cols],
            f1_s.at[k], f1_r.at[sender], (2 * k + c, blk),
        )

    def f1_arrival(k):
        at = fr.at[k, :, pl.ds(0 if k // 2 % 2 == 0 else 384, 640)]
        return remote(at, at, f1_s.at[k], f1_r.at[k], sibling)

    def f2(k, core):
        at = fo.at[pl.ds(pl.multiple_of(16 * q, 16), 16)]
        return remote(at, at, f2_s.at[2 * k + core], f2_r.at[q], (2 * k + core, blk))

    def f2_arrival(k):
        at = fo.at[pl.ds(16 * k, 16)]
        return remote(at, at, f2_s.at[2 * k], f2_r.at[k], sibling)

    @pl.when(is_src)
    def _():
        for half in (0, 1):
            if half:
                rs_local(0, 0, half)
            for side in (0, 1):
                for part in range(RS_PARTS):
                    rs_z(1, side, half, 0, side, side, part).wait_recv()
                add(0, rows(0, half), z_cols, rz, rows(side, half))
            for k in range(4 * half, 4 * half + 4):

                @pl.when(q != k)
                def _():
                    f1(k, q).start()

    @pl.when(is_sink)
    def _():
        for half in (0, 1):
            ag_sink(0, half, (1,))

    use_weight(7)

    @pl.when(is_src)
    def _():
        own_rows = pl.ds(pl.multiple_of(16 * q, 16), 16)
        fr[q, :, z_cols] = ts[0, own_rows, z_cols]
        for k in range(8):
            pl.when(q != k)(lambda: f1_arrival(k).wait_recv())

        def total(keys, cols):
            return sum(fr[k, :, cols].astype(F32) for k in keys)

        even, odd = (0, 1, 4, 5), (2, 3, 6, 7)
        fo[own_rows, pl.ds(0, 384)] = total(even, pl.ds(0, 384)).astype(BF16)
        fo[own_rows, pl.ds(384, 256)] = total(even + odd, pl.ds(384, 256)).astype(BF16)
        fo[own_rows, pl.ds(640, 384)] = total(odd, pl.ds(640, 384)).astype(BF16)
        for k in range(8):
            for core in (0, 1):

                @pl.when((q != k) | (c != core))
                def _():
                    f2(k, core).start()

    use_weight(0, True)

    swap_g.wait_send()

    @pl.loop(0, 8)
    def _(p):
        for side in (0, 1):
            swap_x(p, side).wait_send()
            pg_copy(p, side).wait()

        @pl.when(is_src)
        def _():
            for side in (0, 1):
                for half in (0, 1):
                    ag_x(p, side, half).wait_send()
                    ag_y(p, side, half, src_own).wait_send()
                    rs_y(p, side, half, src_other).wait_send()

                def sent_z(half):
                    for part in range(AG_PARTS):
                        ag_z(p, side, half, p, side, side, part).wait_send()
                    for part in range(RS_PARTS):
                        rs_z(p, side, half, p, side, side, part).wait_send()

                @pl.when((p > 0) | (side == 1))
                def _():
                    sent_z(0)
                    sent_z(1)

        @pl.when(is_sink)
        def _():
            for side in (0, 1):
                for half in (0, 1):
                    ag_y(p, side, half, sink_own).wait_send()
                    rs_y(p, side, half, sink_other).wait_send()
                    rs_x(p, side, half).wait_send()

    theirs_out.wait()
    bo_ref[...] = (acc[pl.ds(0, R)] + bor[...]).astype(BF16)

    @pl.when(is_src)
    def _():
        for k in range(8):
            pl.when(q != k)(lambda: f1(k, q).wait_send())
            for core in (0, 1):

                @pl.when((q != k) | (c != core))
                def _():
                    f2(k, core).wait_send()

    for k in range(8):

        @pl.when((q != k) | is_sink)
        def _():
            f2_arrival(k).wait_recv()


def finish(bo_ref, pg_ref, fo_ref, bo_out, pg_out, wgrad_out, scaled, sem):
    copies = [
        pltpu.make_async_copy(pg_ref, pg_out, sem.at[0]),
        pltpu.make_async_copy(bo_ref, bo_out, sem.at[1]),
        pltpu.make_async_copy(scaled, wgrad_out, sem.at[2]),
    ]
    copies[0].start()
    copies[1].start()
    scaled[...] = fo_ref[...].astype(F32) * (1.0 / math.sqrt(98304))
    copies[2].start()
    for copy in copies:
        copy.wait()


def body(pre_gelu, out_grad, down_weight):
    dma = pltpu.SemaphoreType.DMA
    vmem = pltpu.VMEM
    hbm = pl.BlockSpec(memory_space=pl.ANY)
    whole = pl.BlockSpec(memory_space=vmem)
    results = pl.pallas_call(
        kernel,
        out_shape=(
            jax.ShapeDtypeStruct((R, D), BF16),
            jax.ShapeDtypeStruct((R, 2 * SHARE), BF16),
            jax.ShapeDtypeStruct((BLK, D), BF16),
        ),
        in_specs=[pl.BlockSpec(memory_space=pltpu.HBM)] * 3,
        out_specs=(whole, whole, whole),
        scratch_shapes=[
            vmem((2 * R, SHARE), BF16),
            vmem((8, 2 * R, 256), BF16),
            vmem((8, 2 * R, 256), F32),
            vmem((2 * R, D), BF16),
            vmem((8, 256, D), BF16),
            vmem((8, 256, D), BF16),
            vmem((8, 256, D), BF16),
            vmem((8, 256, D), BF16),
            vmem((8, 256, D), BF16),
            vmem((2 * R, D), F32),
            vmem((R, D), F32),
            vmem((8, R, 256), BF16),
            vmem((8, 16, D), BF16),
            dma((5,)),
            dma((16,)),
            dma((16,)),
            *[dma((32,)) for _ in range(8)],
            *[dma((32 * AG_PARTS,)) for _ in range(2)],
            *[dma((32 * RS_PARTS,)) for _ in range(2)],
            dma((16,)),
            dma((16,)),
            dma((2,)),
            dma((8,)),
            dma((8,)),
            dma((16,)),
            dma((8,)),
        ],
        compiler_params=pltpu.CompilerParams(
            collective_id=0, has_side_effects=True, vmem_limit_bytes=50 * 1024 * 1024
        ),
        cost_estimate=pl.CostEstimate(flops=4831838208, bytes_accessed=4 << 20, transcendentals=786432),
        name="fused",
    )(pre_gelu, out_grad, down_weight)
    return pl.pallas_call(
        finish,
        out_shape=(
            jax.ShapeDtypeStruct((R, D), BF16),
            jax.ShapeDtypeStruct((R, 2 * SHARE), BF16),
            jax.ShapeDtypeStruct((BLK, D), F32),
        ),
        in_specs=[whole, whole, whole],
        out_specs=(hbm, hbm, hbm),
        scratch_shapes=[vmem((BLK, D), F32), dma((3,))],
        compiler_params=pltpu.CompilerParams(vmem_limit_bytes=4 * 1024 * 1024),
        cost_estimate=pl.CostEstimate(flops=131072, bytes_accessed=3 << 20, transcendentals=0),
        name="finish",
    )(*results)


def solution(mesh):
    in_specs = (P(("dp", "blk"), None), P(("dp", "blk"), None), P("blk", None))
    out_specs = (P(("dp", "blk"), None), P(("dp", "blk"), None), P("blk", None))
    return jax.shard_map(body, mesh=mesh, in_specs=in_specs, out_specs=out_specs, check_vma=False)
```

```python
import math

import jax
import jax.numpy as jnp
from jax import lax
from jax.experimental import pallas as pl
from jax.experimental.pallas import tpu as pltpu
from jax.sharding import PartitionSpec as P

MESH = pl.DeviceIdType.MESH
SQRT_TWO_PI = 0.7978845608028654
CUBIC = 0.044715
F32, BF16 = jnp.float32, jnp.bfloat16
R = 192
D = 1024
BLK = 128
HALF = 64
AG_PARTS = 1
RS_PARTS = 2
SHARE = 2048


def gelu_parts(inputs):
    squared = inputs * inputs
    argument = inputs * (SQRT_TWO_PI + (SQRT_TWO_PI * CUBIC) * squared)
    tangent = jnp.tanh(argument)
    gate = 0.5 + 0.5 * tangent
    activation = inputs * gate
    bend = inputs * (0.5 * SQRT_TWO_PI + (1.5 * CUBIC * SQRT_TWO_PI) * squared)
    derivative = gate + (1.0 - tangent * tangent) * bend
    return activation, derivative


def kernel(
    pre_ref, og_ref, w_ref, bo_ref, pg_ref, fo,
    xs, hs, ss, gs, wg, ts, ry, rx, rz, acc, bor, pgs, fr,
    in_sem, sx_s, sx_r, agx_r, agy_r, agx_s, agy_s, rsy_s, rsx_s, rsy_r, rsx_r, agz_s, agz_r, rsz_s, rsz_r,
    pgs_sem, pgr_sem, bo_sem, f1_s, f1_r, f2_s, f2_r,
):
    dp = lax.axis_index("dp")
    blk = lax.axis_index("blk")
    y, xh, c = dp // 4, (dp // 2) % 2, dp % 2
    xl, z = blk // 16, blk % 16
    yp = y % 2
    q = y * 2 + xh
    is_src = c == xl
    is_sink = c != xl

    z_next = [(dp, xl * 16 + (z + 1) % 16), (dp, xl * 16 + (z + 15) % 16)]
    x_same, x_flip = xh * 2, (1 - xh) * 2
    x_blk = (1 - xl) * 16 + z
    x_next = [
        (y * 4 + jnp.where(xl == 0, x_same, x_flip) + c, x_blk),
        (y * 4 + jnp.where(xl == 0, x_flip, x_same) + c, x_blk),
    ]
    y_next = [((y + 1) % 4 * 4 + dp % 4, blk), ((y + 3) % 4 * 4 + dp % 4, blk)]
    sibling = (dp + 1 - 2 * c, blk)

    def pick(pair, down):
        if isinstance(down, int):
            return pair[down]
        return tuple(jnp.where(down == 0, a, b) for a, b in zip(*pair))

    def remote(src, dst, send, recv, device):
        return pltpu.make_async_remote_copy(
            src_ref=src, dst_ref=dst, send_sem=send, recv_sem=recv, device_id=device, device_id_type=MESH
        )

    z_cols = pl.ds(pl.multiple_of(yp * 384, 128), 640)
    x_cols = pl.ds(pl.multiple_of(yp * 384, 128), 640)
    src_own, src_other = (pl.ds(pl.multiple_of(k * 640, 128), 384) for k in (yp, 1 - yp))
    sink_own, sink_other = (pl.ds(pl.multiple_of(k * 640, 128), 384) for k in (yp, 1 - yp))

    mine = pl.ds(pl.multiple_of(c * SHARE, SHARE), SHARE)
    load_x = pltpu.make_async_copy(pre_ref.at[:, mine], xs.at[pl.ds(0, R)], in_sem.at[0])
    load_g = pltpu.make_async_copy(og_ref, gs.at[pl.ds(0, R)], in_sem.at[1])
    load_w = pltpu.make_async_copy(w_ref.at[:, z_cols], wg.at[0, pl.ds(0, BLK), z_cols], in_sem.at[2])

    @pl.when(is_src)
    def _():
        load_w.start()

    load_x.start()
    load_g.start()

    barrier = pltpu.get_barrier_semaphore()
    for peer in z_next + x_next:
        pl.semaphore_signal(barrier, inc=1, device_id=peer, device_id_type=MESH)
    for k in range(16):

        @pl.when(dp != k)
        def _():
            pl.semaphore_signal(barrier, inc=1, device_id=(k, blk), device_id_type=MESH)

    acc[...] = jnp.zeros_like(acc)
    pl.semaphore_wait(barrier, 19)

    def block_columns(p, side):
        far = jnp.where(p == 0, 8, p)
        zb = (z + far) % 16 if side else (z - p + 16) % 16
        return pl.multiple_of(zb * BLK, BLK)

    swap_g = remote(og_ref, gs.at[pl.ds(R, R)], in_sem.at[3], in_sem.at[4], sibling)

    def swap_x(p, side):
        at, k = block_columns(p, side), 2 * p + side
        theirs = pl.ds(pl.multiple_of((1 - c) * SHARE, SHARE) + at, BLK)
        return remote(pre_ref.at[:, theirs], xs.at[pl.ds(R, R), pl.ds(at, BLK)], sx_s.at[k], sx_r.at[k], sibling)

    def rows(side, half):
        return pl.ds(side * BLK + half * HALF, HALF)

    def part_rows(side, half, part, parts):
        return pl.ds(side * BLK + half * HALF + part * (HALF // parts), HALF // parts)

    def unit(p, side, half):
        return 4 * p + 2 * side + half

    def z_to(side):
        return z_next[side]

    def ag_z(p, side, half, to_p, to_side, way, part):
        u = AG_PARTS * unit(to_p, to_side, half) + part
        return remote(
            wg.at[p, part_rows(side, half, part, AG_PARTS), z_cols],
            wg.at[to_p, part_rows(to_side, half, part, AG_PARTS), z_cols],
            agz_s.at[u], agz_r.at[u], z_to(way),
        )

    def ag_x(p, side, half):
        u, at = unit(p, side, half), wg.at[p, rows(side, half), x_cols]
        return remote(at, at, agx_s.at[u], agx_r.at[u], pick(x_next, half))

    def ag_y(p, side, half, cols):
        u, at = unit(p, side, half), wg.at[p, rows(side, half), cols]
        return remote(at, at, agy_s.at[u], agy_r.at[u], pick(y_next, half))

    def ag_src(d, half):
        for part in range(AG_PARTS):
            for side in (0, 1):
                ag_z(d, side, half, d, side, side, part).wait_recv()

                @pl.when(d < 7)
                def _():
                    ag_z(d, side, half, d + 1, side, side, part).start()

                @pl.when((d == 7) & (half == side))
                def _():
                    ag_z(d, side, half, 0, 1, side, part).start()

        for side in (0, 1):
            ag_x(d, side, half).start()
            ag_y(d, side, half, src_own).start()

    def ag_src_last(half):
        for part in range(AG_PARTS):
            ag_z(0, 1, half, 0, 1, half, part).wait_recv()
        ag_x(0, 1, half).start()
        ag_y(0, 1, half, src_own).start()

    def ag_sink(p, half, sides=(0, 1)):
        for side in sides:
            ag_x(p, side, half).wait_recv()
            ag_y(p, side, half, sink_own).start()

    def rs_y(p, side, half, cols):
        u = unit(p, side, half)
        return remote(
            ts.at[p, rows(side, half), cols], ry.at[p, rows(side, half), cols],
            rsy_s.at[u], rsy_r.at[u], pick(y_next, 1 - half),
        )

    def rs_x(p, side, half):
        u = unit(p, side, half)
        return remote(
            ts.at[p, rows(side, half), x_cols], rx.at[p, rows(side, half), x_cols],
            rsx_s.at[u], rsx_r.at[u], pick(x_next, 1 - half),
        )

    def rs_z(p, side, half, to_p, to_side, way, part):
        return remote(
            ts.at[p, part_rows(side, half, part, RS_PARTS), z_cols],
            rz.at[to_p, part_rows(to_side, half, part, RS_PARTS), z_cols],
            rsz_s.at[RS_PARTS * unit(p, side, half) + part],
            rsz_r.at[RS_PARTS * unit(to_p, to_side, half) + part], z_to(1 - way),
        )

    def add(p, at, cols, buffer, from_at=None):
        from_at = at if from_at is None else from_at
        ts[p, at, cols] = ts[p, at, cols] + buffer[p, from_at, cols]

    def rs_y_send(p):
        def send(cols):
            for side in (0, 1):
                for half in (0, 1):
                    rs_y(p, side, half, cols).start()

        pl.when(is_src)(lambda: send(src_other))
        pl.when(is_sink)(lambda: send(sink_other))

    def rs_sink(p, side, half):
        rs_y(p, side, half, sink_own).wait_recv()
        add(p, rows(side, half), sink_own, ry)
        rs_x(p, side, half).start()

    def rs_local(p, side, half):
        rs_y(p, side, half, src_own).wait_recv()
        add(p, rows(side, half), src_own, ry)
        rs_x(p, side, half).wait_recv()
        add(p, rows(side, half), x_cols, rx)

    def rs_src(p, half):
        for part in range(RS_PARTS):
            for side in (0, 1):

                @pl.when((p < 7) | (half != side))
                def _():
                    rs_z(p, side, half, p, side, side, part).wait_recv()
                    add(p, part_rows(side, half, part, RS_PARTS), z_cols, rz)

                rs_z(p, side, half, p - 1, side, side, part).start()

    def rs_src_first(half):
        rs_local(0, 1, half)
        for part in range(RS_PARTS):
            rs_z(0, 1, half, 7, 1 - half, 1 - half, part).start()

    def hidden(p):
        for side in (0, 1):
            cols = pl.ds(block_columns(p, side), BLK)

            @pl.loop(0, 2 * R // 64)
            def _(i):
                at = pl.ds(pl.multiple_of(i * 64, 64), 64)
                activation, derivative = gelu_parts(xs[at, cols].astype(F32))
                hs[p, at, pl.ds(side * BLK, BLK)] = activation.astype(BF16)
                ss[p, at, pl.ds(side * BLK, BLK)] = derivative

    def term(p):
        turned = hs[p].T
        for n in range(4):
            cols = pl.ds(n * 256, 256)
            ts[p, :, cols] = jnp.dot(turned, gs[:, cols], preferred_element_type=F32).astype(BF16)

    def pg_columns(p, side):
        return pl.ds(pl.multiple_of(c * SHARE, SHARE) + block_columns(p, side), BLK)

    def pg_copy(p, side):
        k = 2 * p + side
        part = pgs.at[p, :, pl.ds(side * BLK, BLK)]
        return remote(part, pg_ref.at[:, pg_columns(p, side)], pgs_sem.at[k], pgr_sem.at[k], sibling)

    theirs_out = remote(acc.at[pl.ds(R, R)], bor, bo_sem.at[0], bo_sem.at[1], sibling)

    def use_weight(p, last=False):
        def arrive(cols):
            for side in (0, 1):
                for half in (0, 1):
                    ag_y(p, side, half, cols).wait_recv()

        pl.when(is_src)(lambda: arrive(src_other))
        pl.when(is_sink)(lambda: arrive(sink_other))
        weight = wg.at[p]

        def add_out(at):
            for n in range(4):
                cols = pl.ds(n * 256, 256)
                acc[at, cols] += jnp.dot(hs[p, at, :], weight[:, cols], preferred_element_type=F32)

        if last:
            add_out(pl.ds(R, R))
            theirs_out.start()
        d_hidden = lax.dot_general(gs[...], weight[...], (((1,), (1,)), ((), ())), preferred_element_type=F32)
        grads = (d_hidden * ss[p]).astype(BF16)
        pgs[p] = grads[R:]
        for side in (0, 1):
            pg_copy(p, side).start()
        for side in (0, 1):
            pg_ref[:, pg_columns(p, side)] = grads[:R, side * BLK : (side + 1) * BLK]
        add_out(pl.ds(0, R) if last else pl.ds(0, 2 * R))

    @pl.when(is_src)
    def _():
        load_w.wait()
        for half in (0, 1):
            for part in range(AG_PARTS):
                ag_z(0, 0, half, 1, 0, 0, part).start()
                ag_z(0, 0, half, 1, 1, 1, part).start()

    swap_x(0, 0).start()
    swap_x(0, 1).start()
    swap_g.start()

    @pl.loop(1, 8)
    def _(s):
        swap_x(8 - s, 0).start()
        swap_x(8 - s, 1).start()

    @pl.when(is_src)
    def _():
        for half in (0, 1):
            ag_x(0, 0, half).start()
            ag_y(0, 0, half, src_own).start()

    load_x.wait()
    load_g.wait()

    @pl.loop(0, 8)
    def _(s):
        p = (8 - s) % 8
        swap_x(p, 0).wait_recv()
        swap_x(p, 1).wait_recv()
        hidden(p)

        @pl.when(s == 0)
        def _():
            swap_g.wait_recv()

        term(p)
        rs_y_send(p)

        @pl.when((s >= 2) & is_sink)
        def _():
            before = (10 - s) % 8
            for half in (0, 1):
                for side in (0, 1):
                    rs_sink(before, side, half)

        @pl.when((s == 6) & is_src)
        def _():
            for half in (0, 1):
                rs_src_first(half)

        @pl.when((s > 2) & (s % 2 == 1) & is_src)
        def _():
            m = (s - 3) // 2
            ag_src(1 + m // 2, m % 2)

        @pl.when((s == 5) & is_sink)
        def _():
            for half in (0, 1):
                ag_sink(0, half, (0,))

        @pl.when((s == 7) & is_sink)
        def _():
            ag_sink(1, 0)

    @pl.when(is_src)
    def _():
        for side in (0, 1):
            rs_local(7, side, 0)

    @pl.loop(2, 16)
    def _(n):
        @pl.when(is_src)
        def _():
            rs_src(8 - n // 2, n % 2)
            later = 7 - (n - 1) // 2
            rs_local(later, 0, (n + 1) % 2)

            @pl.when(later > 0)
            def _():
                rs_local(later, 1, (n + 1) % 2)

        @pl.when((n < 4) & is_sink)
        def _():
            for half in (0, 1):
                for side in (0, 1):
                    rs_sink(4 - n, side, half)

        @pl.when((n < 13) & is_src)
        def _():
            ag_src((n + 3) // 2, (n + 1) % 2)

        @pl.when((n < 15) & is_sink)
        def _():
            ag_sink((n + 1) // 2, (n + 1) % 2)

        @pl.when((n == 14) & is_src)
        def _():
            for half in (0, 1):
                ag_src_last(half)

        @pl.when((n % 2 == 1) & (n > 4))
        def _():
            use_weight((n - 3) // 2)

    def f1(k, sender):
        return remote(
            ts.at[0, pl.ds(16 * k, 16), z_cols], fr.at[sender, :, z_cols],
            f1_s.at[k], f1_r.at[sender], (2 * k + c, blk),
        )

    def f1_arrival(k):
        at = fr.at[k, :, pl.ds(0 if k // 2 % 2 == 0 else 384, 640)]
        return remote(at, at, f1_s.at[k], f1_r.at[k], sibling)

    def f2(k, core):
        at = fo.at[pl.ds(pl.multiple_of(16 * q, 16), 16)]
        return remote(at, at, f2_s.at[2 * k + core], f2_r.at[q], (2 * k + core, blk))

    def f2_arrival(k):
        at = fo.at[pl.ds(16 * k, 16)]
        return remote(at, at, f2_s.at[2 * k], f2_r.at[k], sibling)

    @pl.when(is_src)
    def _():
        for half in (0, 1):
            if half:
                rs_local(0, 0, half)
            for side in (0, 1):
                for part in range(RS_PARTS):
                    rs_z(1, side, half, 0, side, side, part).wait_recv()
                add(0, rows(0, half), z_cols, rz, rows(side, half))
            for k in range(4 * half, 4 * half + 4):

                @pl.when(q != k)
                def _():
                    f1(k, q).start()

    @pl.when(is_sink)
    def _():
        for half in (0, 1):
            ag_sink(0, half, (1,))

    use_weight(7)

    @pl.when(is_src)
    def _():
        own_rows = pl.ds(pl.multiple_of(16 * q, 16), 16)
        fr[q, :, z_cols] = ts[0, own_rows, z_cols]
        for k in range(8):
            pl.when(q != k)(lambda: f1_arrival(k).wait_recv())

        def total(keys, cols):
            return sum(fr[k, :, cols].astype(F32) for k in keys)

        even, odd = (0, 1, 4, 5), (2, 3, 6, 7)
        fo[own_rows, pl.ds(0, 384)] = total(even, pl.ds(0, 384)).astype(BF16)
        fo[own_rows, pl.ds(384, 256)] = total(even + odd, pl.ds(384, 256)).astype(BF16)
        fo[own_rows, pl.ds(640, 384)] = total(odd, pl.ds(640, 384)).astype(BF16)
        for k in range(8):
            for core in (0, 1):

                @pl.when((q != k) | (c != core))
                def _():
                    f2(k, core).start()

    use_weight(0, True)

    swap_g.wait_send()

    @pl.loop(0, 8)
    def _(p):
        for side in (0, 1):
            swap_x(p, side).wait_send()
            pg_copy(p, side).wait()

        @pl.when(is_src)
        def _():
            for side in (0, 1):
                for half in (0, 1):
                    ag_x(p, side, half).wait_send()
                    ag_y(p, side, half, src_own).wait_send()
                    rs_y(p, side, half, src_other).wait_send()

                def sent_z(half):
                    for part in range(AG_PARTS):
                        ag_z(p, side, half, p, side, side, part).wait_send()
                    for part in range(RS_PARTS):
                        rs_z(p, side, half, p, side, side, part).wait_send()

                @pl.when((p > 0) | (side == 1))
                def _():
                    sent_z(0)
                    sent_z(1)

        @pl.when(is_sink)
        def _():
            for side in (0, 1):
                for half in (0, 1):
                    ag_y(p, side, half, sink_own).wait_send()
                    rs_y(p, side, half, sink_other).wait_send()
                    rs_x(p, side, half).wait_send()

    theirs_out.wait()
    bo_ref[...] = (acc[pl.ds(0, R)] + bor[...]).astype(BF16)

    @pl.when(is_src)
    def _():
        for k in range(8):
            pl.when(q != k)(lambda: f1(k, q).wait_send())
            for core in (0, 1):

                @pl.when((q != k) | (c != core))
                def _():
                    f2(k, core).wait_send()

    for k in range(8):

        @pl.when((q != k) | is_sink)
        def _():
            f2_arrival(k).wait_recv()


def finish(bo_ref, pg_ref, fo_ref, bo_out, pg_out, wgrad_out, scaled, sem):
    copies = [
        pltpu.make_async_copy(pg_ref, pg_out, sem.at[0]),
        pltpu.make_async_copy(bo_ref, bo_out, sem.at[1]),
        pltpu.make_async_copy(scaled, wgrad_out, sem.at[2]),
    ]
    copies[0].start()
    copies[1].start()
    scaled[...] = fo_ref[...].astype(F32) * (1.0 / math.sqrt(98304))
    copies[2].start()
    for copy in copies:
        copy.wait()


def body(pre_gelu, out_grad, down_weight):
    dma = pltpu.SemaphoreType.DMA
    vmem = pltpu.VMEM
    hbm = pl.BlockSpec(memory_space=pl.ANY)
    whole = pl.BlockSpec(memory_space=vmem)
    inputs = [pltpu.with_memory_space_constraint(a, pltpu.HBM) for a in (pre_gelu, out_grad, down_weight)]
    results = pl.pallas_call(
        kernel,
        out_shape=(
            jax.ShapeDtypeStruct((R, D), BF16),
            jax.ShapeDtypeStruct((R, 2 * SHARE), BF16),
            jax.ShapeDtypeStruct((BLK, D), BF16),
        ),
        in_specs=[pl.BlockSpec(memory_space=pltpu.HBM)] * 3,
        out_specs=(whole, whole, whole),
        scratch_shapes=[
            vmem((2 * R, SHARE), BF16),
            vmem((8, 2 * R, 256), BF16),
            vmem((8, 2 * R, 256), F32),
            vmem((2 * R, D), BF16),
            vmem((8, 256, D), BF16),
            vmem((8, 256, D), BF16),
            vmem((8, 256, D), BF16),
            vmem((8, 256, D), BF16),
            vmem((8, 256, D), BF16),
            vmem((2 * R, D), F32),
            vmem((R, D), F32),
            vmem((8, R, 256), BF16),
            vmem((8, 16, D), BF16),
            dma((5,)),
            dma((16,)),
            dma((16,)),
            *[dma((32,)) for _ in range(8)],
            *[dma((32 * AG_PARTS,)) for _ in range(2)],
            *[dma((32 * RS_PARTS,)) for _ in range(2)],
            dma((16,)),
            dma((16,)),
            dma((2,)),
            dma((8,)),
            dma((8,)),
            dma((16,)),
            dma((8,)),
        ],
        compiler_params=pltpu.CompilerParams(
            collective_id=0, has_side_effects=True, vmem_limit_bytes=50 * 1024 * 1024
        ),
        cost_estimate=pl.CostEstimate(flops=4831838208, bytes_accessed=4 << 20, transcendentals=786432),
        name="fused",
    )(*inputs)
    return pl.pallas_call(
        finish,
        out_shape=(
            jax.ShapeDtypeStruct((R, D), BF16),
            jax.ShapeDtypeStruct((R, 2 * SHARE), BF16),
            jax.ShapeDtypeStruct((BLK, D), F32),
        ),
        in_specs=[whole, whole, whole],
        out_specs=(hbm, hbm, hbm),
        scratch_shapes=[vmem((BLK, D), F32), dma((3,))],
        compiler_params=pltpu.CompilerParams(vmem_limit_bytes=4 * 1024 * 1024),
        cost_estimate=pl.CostEstimate(flops=131072, bytes_accessed=3 << 20, transcendentals=0),
        name="finish",
    )(*results)


def solution(mesh):
    in_specs = (P(("dp", "blk"), None), P(("dp", "blk"), None), P("blk", None))
    out_specs = (P(("dp", "blk"), None), P(("dp", "blk"), None), P("blk", None))
    return jax.shard_map(body, mesh=mesh, in_specs=in_specs, out_specs=out_specs, check_vma=False)
```
